32 devices in a mesh: dp: 8 (over y, x, core), tensor: 4 (over z).
Axes of the slice: x: 2, y: 2, z: 4, core: 2. Of those that a mesh axis runs over, the one named last changes fastest.
Arguments:
- target_hidden: bfloat16 [256, 16384], P('dp', 'tensor'), may hold values from -64 to 64
- target_gain: bfloat16 [16384], replicated, may hold values from 0.25 to 1.75
- target_head: bfloat16 [16384, 65536], P(None, ('dp', 'tensor')), may hold values from -8 to 8
- reference_hidden: bfloat16 [256, 4096], P('dp', 'tensor'), may hold values from -64 to 64
- reference_gain: bfloat16 [4096], replicated, may hold values from 0.25 to 1.75
- reference_head: bfloat16 [4096, 65536], P(None, ('dp', 'tensor')), may hold values from -8 to 8
Outputs:
- contrast: float32 [256, 65536], P(None, ('dp', 'tensor'))
The draws below stay inside these ranges and needn't reach their ends.
All inputs are finite; a program needn't handle non-finite values.
Results may differ from the reference program's by a relative error of at most 0.0012.
Values may be sent and summed in bfloat16 or wider, within the bound.
A program may use at most 192 MiB of HBM per device.

```python
import jax
import jax.numpy as jnp
from jax import lax

ROWS = 256
D = 16384
DR = 4096
V = 65536


def head_matrix(key, width, columns):

    def one_column(column):
        column_key = jax.random.fold_in(key, column)
        values = jnp.clip(jax.random.normal(column_key, (width,), jnp.float32), -6.0, 6.0)
        wobble = jax.random.uniform(jax.random.fold_in(column_key, 7), (), jnp.float32, -0.3, 0.3)
        factor = 3.0 * jnp.exp2(column.astype(jnp.float32) / V) * jnp.exp(wobble)
        return values * factor / jnp.sqrt(jnp.float32(width))
    return jnp.clip(jax.vmap(one_column)(columns).T, -8.0, 8.0)


def hidden_rows(key, width, count):
    keys = jax.random.split(key, 2)
    column_scale = jnp.power(10.0, jnp.arange(width, dtype=jnp.float32) / width)[None, :]
    row_scale = jnp.power(10.0, jax.random.uniform(keys[1], (count, 1), jnp.float32))
    base = jnp.clip(jax.random.normal(keys[0], (count, width), jnp.float32), -6.0, 6.0)
    values = 0.2 * base * row_scale * column_scale
    return jnp.clip(values, -64.0, 64.0)


def draw_target_head(key, part):
    return head_matrix(jax.random.fold_in(key, 21), D, jnp.arange(V)).astype(jnp.bfloat16)


def draw_reference_head(key, part):
    return head_matrix(jax.random.fold_in(key, 31), DR, jnp.arange(V)).astype(jnp.bfloat16)


def draw_target_hidden(key, part):
    return hidden_rows(jax.random.fold_in(key, 22), D, ROWS).astype(jnp.bfloat16)


def draw_reference_hidden(key, part):
    return hidden_rows(jax.random.fold_in(key, 32), DR, ROWS).astype(jnp.bfloat16)


def setup_inputs(seed: int = 0) -> dict:
    key_list = jax.random.split(jax.random.key(seed), 7)
    return {
        "target_hidden": draw_target_hidden(jax.random.fold_in(key_list[6], 71), 0),
        "target_gain": jnp.clip(1.0 + 0.15 * jax.random.normal(key_list[1], (D,), jnp.float32), 0.25, 1.75).astype(jnp.bfloat16),
        "target_head": draw_target_head(jax.random.fold_in(key_list[6], 71), 0),
        "reference_hidden": draw_reference_hidden(jax.random.fold_in(key_list[6], 71), 0),
        "reference_gain": jnp.clip(1.0 + 0.15 * jax.random.normal(key_list[4], (DR,), jnp.float32), 0.25, 1.75).astype(jnp.bfloat16),
        "reference_head": draw_reference_head(jax.random.fold_in(key_list[6], 71), 0),
    }


EPS = 1e-05
LOG_TEN = 2.302585092994046

def model_parts(hidden, gain, head):
    values = hidden.astype(jnp.float32)
    square_mean = lax.optimization_barrier(jnp.mean(values * values, axis=1, keepdims=True))
    normed = (values * lax.rsqrt(square_mean + EPS) * gain.astype(jnp.float32)).astype(jnp.bfloat16)
    logits = jnp.dot(normed, head, preferred_element_type=jnp.float32)
    peak = lax.optimization_barrier(jnp.max(logits, axis=1, keepdims=True))
    total = lax.optimization_barrier(jnp.sum(jnp.exp(logits - peak), axis=1, keepdims=True))
    return (logits, peak, peak + jnp.log(total))

def reference(target_hidden, target_gain, target_head, reference_hidden, reference_gain, reference_head):
    target_logits, target_peak, target_lse = model_parts(target_hidden, target_gain, target_head)
    reference_logits, reference_peak, reference_lse = model_parts(reference_hidden, reference_gain, reference_head)
    margin = jnp.minimum(0.0, target_logits - target_peak + LOG_TEN)
    return target_logits - target_lse - 0.5 * (reference_logits - reference_lse) + margin
```

```python
import functools

import jax
import jax.numpy as jnp
from jax import lax
from jax.experimental import pallas as pl
from jax.experimental.pallas import tpu as pltpu
from jax.sharding import PartitionSpec as P

EPS = 1e-05
LOG_TEN = 2.302585092994046
MESH = pl.DeviceIdType.MESH
F32 = jnp.float32


def kernel(
    n_dp, n_t, nw, ht_ref, hr_ref, gain_ref, wt_ref, wr_ref, out_ref,
    normed, heads, acc_t, acc_r, local_stats, squares, squares_in, stat_a, stat_b,
    z_send, z_recv, two_send, two_recv, three_send, three_recv, core_send, core_recv,
    sq_send, sq_recv, a_send, a_recv, b_send, b_recv, head_sem, out_sem,
):
    quads = n_dp // 2
    n_lo, n_hi = 2, quads // 2
    half = normed.shape[3]
    width = normed.shape[4]
    rows = n_dp * 2 * half
    columns = acc_t.shape[1]
    d = lax.axis_index("dp")
    z = lax.axis_index("tensor")
    core = lax.rem(d, 2)
    lo = lax.rem(lax.div(d, 2), n_lo)
    hi = lax.div(d, 2 * n_lo)
    base_a = core * quads
    base_b = n_dp + core * quads
    own_a = base_a + hi * n_lo + lo
    own_b = base_b + lo * n_hi + hi

    def dp_index(high, low, c):
        return (high * n_lo + low) * 2 + c

    sibling = dp_index(hi, lo, 1 - core)
    other_lo = [lax.rem(lo + k, n_lo) for k in range(1, n_lo)]
    other_hi = [lax.rem(hi + k, n_hi) for k in range(1, n_hi)]
    other_z = [lax.rem(z + k, n_t) for k in range(1, n_t)]
    other_d = [lax.rem(d + k, n_dp) for k in range(1, n_dp)]

    def send(src, dst, send_sem, recv_sem, dev):
        pltpu.make_async_remote_copy(
            src_ref=src, dst_ref=dst, send_sem=send_sem, recv_sem=recv_sem,
            device_id=dev, device_id_type=MESH,
        ).start()

    def push(view, send_sem, recv_sem, dev):
        send(view, view, send_sem, recv_sem, dev)

    def await_bytes(view, sem):
        pltpu.make_async_copy(view, view, sem).wait()

    def head_copy(j, i):
        slot = j % 2
        if j == 0:
            src = wr_ref.at[pl.ds(pl.multiple_of(i * width, width), width), :]
        else:
            src = wt_ref.at[pl.ds(pl.multiple_of((i * (nw - 1) + j - 1) * width, width), width), :]
        return pltpu.make_async_copy(src, heads.at[slot, i], head_sem.at[slot, i])

    def start_heads(j):
        def body(i, _):
            head_copy(j, i).start()
            return 0
        lax.fori_loop(0, n_t, body, 0)

    start_heads(0)
    start_heads(1)

    barrier = pltpu.get_barrier_semaphore()
    for t in other_z:
        pl.semaphore_signal(barrier, inc=1, device_id=(d, t), device_id_type=MESH)
    for p in other_d:
        pl.semaphore_signal(barrier, inc=1, device_id=(p, z), device_id_type=MESH)

    vt = ht_ref[...].astype(F32)
    vr = hr_ref[...].astype(F32)
    st = jnp.sum(vt * vt, axis=1, keepdims=True)
    sr = jnp.sum(vr * vr, axis=1, keepdims=True)
    lane = lax.broadcasted_iota(jnp.int32, squares.shape, 1)
    squares[...] = jnp.where(lane < 64, st, sr)
    squares_in[z] = squares[...]
    pl.semaphore_wait(barrier, n_t + n_dp - 2)
    for t in other_z:
        send(squares, squares_in.at[z], sq_send, sq_recv, (d, t))
    await_bytes(squares_in.at[pl.ds(0, n_t - 1)], sq_recv)
    total_sq = squares_in[0]
    for k in range(1, n_t):
        total_sq = total_sq + squares_in[k]
    scale_t = lax.rsqrt(total_sq[:, 0:1] / F32(width * (nw - 1) * n_t) + EPS)
    scale_r = lax.rsqrt(total_sq[:, 64:65] / F32(width * n_t) + EPS)

    def normalize(j):
        gain = gain_ref[:, j * width:(j + 1) * width]
        if j == 0:
            part, scale = hr_ref[...], scale_r
        else:
            part, scale = ht_ref[:, (j - 1) * width:j * width], scale_t
        value = (part.astype(F32) * scale * gain).astype(jnp.bfloat16)
        normed[j, z, own_a] = value[:half]
        normed[j, z, own_b] = value[half:]

    def start_z(j):
        for t in other_z:
            push(normed.at[j, z, own_a], z_send, z_recv.at[j], (d, t))
            push(normed.at[j, z, own_b], z_send, z_recv.at[j], (d, t))

    def to_core(view, j):
        push(view, core_send, core_recv.at[j], (sibling, z))

    def start_two(j):
        for x in other_lo:
            push(normed.at[j, :, own_a], two_send, two_recv.at[j], (dp_index(hi, x, core), z))
        for y in other_hi:
            push(normed.at[j, :, own_b], two_send, two_recv.at[j], (dp_index(y, lo, core), z))
        to_core(normed.at[j, :, own_a], j)
        to_core(normed.at[j, :, own_b], j)

    def start_three(j):
        for y in other_hi:
            push(normed.at[j, :, pl.ds(base_a + hi * n_lo, n_lo)], three_send, three_recv.at[j],
                 (dp_index(y, lo, core), z))
        for x in other_lo:
            push(normed.at[j, :, pl.ds(base_b + lo * n_hi, n_hi)], three_send, three_recv.at[j],
                 (dp_index(hi, x, core), z))
        for x in other_lo:
            to_core(normed.at[j, :, base_a + hi * n_lo + x], j)
        for y in other_hi:
            to_core(normed.at[j, :, base_b + lo * n_hi + y], j)

    def finish_three(j):
        for y in other_hi:
            to_core(normed.at[j, :, pl.ds(base_a + y * n_lo, n_lo)], j)
        for x in other_lo:
            to_core(normed.at[j, :, pl.ds(base_b + x * n_hi, n_hi)], j)

    tile = min(512, columns)

    def multiply(j):
        acc = acc_r if j == 0 else acc_t

        def one(i, _):
            head_copy(j, i).wait()

            def part(n, _):
                cols = pl.ds(pl.multiple_of(n * tile, tile), tile)
                product = jnp.dot(
                    normed[j, i].reshape(rows, width), heads[j % 2, i, :, cols],
                    preferred_element_type=F32,
                )
                acc[:, cols] += product
                return 0

            lax.fori_loop(0, columns // tile, part, 0)
            if j + 2 < nw:
                head_copy(j + 2, i).start()
            return 0

        acc[...] = jnp.zeros_like(acc)if j < 2 else acc[...]
        lax.fori_loop(0, n_t, one, 0)

    lanes = lax.broadcasted_iota(jnp.int32, (half, 128), 1)

    def row_stats(acc, first):
        def body(b, _):
            r = pl.ds(pl.multiple_of(b * half, half), half)
            v = acc[r, :]
            peak = jnp.max(v, axis=1, keepdims=True)
            total = jnp.sum(jnp.exp(v - peak), axis=1, keepdims=True)
            old = local_stats[r, :]
            local_stats[r, :] = jnp.where(
                lanes == first, peak, jnp.where(lanes == first + 1, total, old)
            )
            return 0

        lax.fori_loop(0, 2 * n_dp, body, 0)

    local_stats[...] = jnp.zeros_like(local_stats)
    normalize(0)
    start_z(0)
    for j in range(1, nw):
        normalize(j)

    for s in range(nw + 3):
        if 0 <= s - 1 < nw:
            j = s - 1
            await_bytes(normed.at[j, :, pl.ds(0, n_lo + n_hi - 2)], two_recv.at[j])
            start_three(j)
        if s < nw:
            await_bytes(normed.at[s, pl.ds(0, n_t - 1), pl.ds(0, 2)], z_recv.at[s])
            start_two(s)
            if s + 1 < nw:
                start_z(s + 1)
        if 0 <= s - 3 < nw:
            j = s - 3
            await_bytes(normed.at[j, :, pl.ds(0, n_dp)], core_recv.at[j])
            multiply(j)
            if j == 0:
                row_stats(acc_r, 2)
        if 0 <= s - 2 < nw:
            j = s - 2
            await_bytes(
                normed.at[j, :, pl.ds(0, n_lo * (n_hi - 1) + n_hi * (n_lo - 1))], three_recv.at[j]
            )
            finish_three(j)

    row_stats(acc_t, 0)

    def combine(parts):
        peak_t, total_t, peak_r, total_r = (
            [p[k:k + 1, :] for p in parts] for k in range(4)
        )
        top_t = functools.reduce(jnp.maximum, peak_t)
        top_r = functools.reduce(jnp.maximum, peak_r)
        sum_t = sum(t * jnp.exp(p - top_t) for p, t in zip(peak_t, total_t))
        sum_r = sum(t * jnp.exp(p - top_r) for p, t in zip(peak_r, total_r))
        return top_t, sum_t, top_r, sum_r

    def stack(values):
        row = lax.broadcasted_iota(jnp.int32, (8, rows), 0)
        result = jnp.zeros((8, rows), F32)
        for k, v in enumerate(values):
            result = jnp.where(row == k, v, result)
        return result

    stat_a[z] = jnp.transpose(local_stats[...])[0:8, :]
    for t in other_z:
        push(stat_a.at[z], a_send, a_recv, (d, t))
    await_bytes(stat_a.at[pl.ds(0, n_t - 1)], a_recv)
    stat_b[d] = stack(combine([stat_a[k] for k in range(n_t)]))
    for p in other_d:
        push(stat_b.at[d], b_send, b_recv, (p, z))
    await_bytes(stat_b.at[pl.ds(0, n_dp - 1)], b_recv)
    top_t, sum_t, top_r, sum_r = combine([stat_b[k] for k in range(n_dp)])
    lse_t = top_t + jnp.log(sum_t)
    lse_r = top_r + jnp.log(sum_r)
    final = stack((top_t, lse_t, lse_r))
    local_stats[...] = jnp.transpose(
        jnp.concatenate([final, jnp.zeros((120, rows), F32)], axis=0)
    )

    def finish(b, place):
        r = pl.ds(pl.multiple_of(b * half, half), half)
        stats = local_stats[r, :]
        lt = acc_t[r, :]
        margin = jnp.minimum(0.0, lt - stats[:, 0:1] + LOG_TEN)
        acc_t[r, :] = lt - stats[:, 1:2] - 0.5 * (acc_r[r, :] - stats[:, 2:3]) + margin
        pltpu.make_async_copy(
            acc_t.at[r, :], out_ref.at[pl.ds(pl.multiple_of(place * half, half), half), :], out_sem
        ).start()

    def finish_a(b, _):
        c, q = b // quads, b % quads
        finish(b, (q * 2 + c) * 2)
        return 0

    def finish_b(b, _):
        c, q = b // quads, b % quads
        low, high = q // n_hi, q % n_hi
        finish(n_dp + b, dp_index(high, low, c) * 2 + 1)
        return 0

    lax.fori_loop(0, n_dp, finish_a, 0)
    lax.fori_loop(0, n_dp, finish_b, 0)

    await_bytes(squares_in.at[pl.ds(0, n_t - 1)], sq_send)
    await_bytes(normed.at[:, pl.ds(0, n_t - 1), pl.ds(0, 2)], z_send)
    await_bytes(normed.at[:, :, pl.ds(0, n_lo + n_hi - 2)], two_send)
    await_bytes(
        normed.at[:, :, pl.ds(0, n_lo * (n_hi - 1) + n_hi * (n_lo - 1))], three_send
    )
    await_bytes(normed.at[:, :, pl.ds(0, n_dp)], core_send)
    await_bytes(stat_a.at[pl.ds(0, n_t - 1)], a_send)
    await_bytes(stat_b.at[pl.ds(0, n_dp - 1)], b_send)
    await_bytes(acc_t, out_sem)


def local(n_dp, n_t, target_hidden, target_gain, target_head, reference_hidden, reference_gain, reference_head):
    rows, wide = target_hidden.shape
    width = reference_hidden.shape[1]
    nw = wide // width + 1
    columns = target_head.shape[1]
    half = rows // 2
    z = lax.axis_index("tensor")
    gain = jnp.concatenate(
        [
            lax.dynamic_slice(reference_gain, (z * width,), (width,)),
            lax.dynamic_slice(target_gain, (z * wide,), (wide,)),
        ]
    ).astype(F32)[None, :]
    dma = pltpu.SemaphoreType.DMA
    vmem = pl.BlockSpec(memory_space=pltpu.VMEM)
    hbm = pl.BlockSpec(memory_space=pl.ANY)
    all_rows = rows * n_dp
    depth = target_head.shape[0] + reference_head.shape[0]
    return pl.pallas_call(
        functools.partial(kernel, n_dp, n_t, nw),
        out_shape=jax.ShapeDtypeStruct((all_rows, columns), F32),
        in_specs=[vmem, vmem, vmem, hbm, hbm],
        out_specs=hbm,
        scratch_shapes=[
            pltpu.VMEM((nw, n_t, 2 * n_dp, half, width), jnp.bfloat16),
            pltpu.VMEM((2, n_t, width, columns), jnp.bfloat16),
            pltpu.VMEM((all_rows, columns), F32),
            pltpu.VMEM((all_rows, columns), F32),
            pltpu.VMEM((all_rows, 128), F32),
            pltpu.VMEM((rows, 128), F32),
            pltpu.VMEM((n_t, rows, 128), F32),
            pltpu.VMEM((n_t, 8, all_rows), F32),
            pltpu.VMEM((n_dp, 8, all_rows), F32),
            dma, dma((nw,)), dma, dma((nw,)), dma, dma((nw,)), dma, dma((nw,)),
            dma, dma, dma, dma, dma, dma, dma((2, n_t)), dma,
        ],
        compiler_params=pltpu.CompilerParams(
            collective_id=0, has_side_effects=True, vmem_limit_bytes=58 * 2**20
        ),
        cost_estimate=pl.CostEstimate(
            flops=2 * all_rows * depth * columns,
            bytes_accessed=2 * depth * columns,
            transcendentals=2 * all_rows * columns,
        ),
    )(target_hidden, reference_hidden, gain, target_head, reference_head)


def solution(mesh):
    placed = (
        P("dp", "tensor"),
        P(),
        P(None, ("dp", "tensor")),
        P("dp", "tensor"),
        P(),
        P(None, ("dp", "tensor")),
    )
    return jax.shard_map(
        functools.partial(local, mesh.shape["dp"], mesh.shape["tensor"]),
        mesh=mesh, in_specs=placed, out_specs=P(None, ("dp", "tensor")), check_vma=False,
    )
```
